256 devices in a mesh: row: 4 (over y), col: 16 (over z, core), layer: 4 (over x).
Axes of the slice: x: 4, y: 4, z: 8, core: 2. Of those that a mesh axis runs over, the one named last changes fastest.
Arguments:
- density: float32 [4096, 4096], P('row', 'col'), may hold values from -1 to 1, as said below
- pattern: int32 [64, 64], replicated, may hold values from 0 to 1, as said below
Outputs:
- purified: float32 [4096, 4096], P('row', 'col')
- traces: float32 [2], replicated
The draws below stay inside these ranges and needn't reach their ends.
Inputs may be any that keep to these rules, and one draw needn't show every extreme that they name: pattern is symmetric and is 1 on the block diagonal and next to it. density is symmetric and zero outside the blocks that pattern keeps.
All inputs are finite; a program needn't handle non-finite values.
Results may differ from the reference program's by a relative error of at most 0.0003.
Values sent between devices are 32-bit elements; how exact they have to be, the bound alone decides.
No kernel may reach another device: no remote copies, remote signals or barrier semaphores. Data moves between devices by JAX's collectives and lax.ppermute only.
A program may use at most 64 MiB of HBM per device.

```python
import jax
import jax.numpy as jnp
from jax import lax

BS = 64
NBLK = 64
STEPS = 2


def block_pattern(key):
    base_key = jax.random.fold_in(key, 11)
    level_key, roll_key = jax.random.split(base_key)
    levels = jax.random.randint(level_key, (NBLK,), 0, 5)
    rolled = jax.random.randint(roll_key, (NBLK, NBLK), 0, 100)
    blocks = jnp.arange(NBLK)
    near_band = jnp.abs(blocks[:, None] - blocks[None, :]) <= 1
    limits = 6 * (levels[:, None] + levels[None, :])
    upper_part = (rolled < limits) & (blocks[:, None] < blocks[None, :])
    kept = near_band | upper_part | upper_part.T
    return kept.astype(jnp.int32)


def draw_pattern(key, part):
    return block_pattern(key)


def draw_density(key, part):
    kept = block_pattern(key)
    counts = jnp.sum(kept, axis=1)
    occupied = jnp.repeat(jnp.repeat(kept, BS, axis=0), BS, axis=1) > 0
    row_counts = jnp.repeat(counts, BS).astype(jnp.float32)
    own_key = jax.random.fold_in(key, 23)
    value_key = jax.random.fold_in(own_key, 0)
    diag_key = jax.random.fold_in(own_key, 2)
    order_size = BS * NBLK
    position = jnp.arange(order_size).astype(jnp.float32) / order_size
    values = jax.random.uniform(value_key, (order_size, order_size), jnp.float32, -1.0, 1.0)
    amplitude = 0.5
    diag_values = 0.15 + 0.55 * position + 0.15 * jax.random.uniform(diag_key, (order_size,), jnp.float32)
    symmetric = 0.5 * (values + values.T)
    spread = amplitude / jnp.sqrt(BS * jnp.maximum(row_counts[:, None], row_counts[None, :]))
    off_part = jnp.where(occupied, symmetric * spread, 0.0)
    indices = jnp.arange(order_size)
    on_diag = indices[:, None] == indices[None, :]
    return jnp.where(on_diag, jnp.broadcast_to(diag_values[:, None], (order_size, order_size)), off_part).astype(jnp.float32)


def setup_inputs(seed: int = 0) -> dict:
    keys = jax.random.split(jax.random.key(seed), 3)
    density = draw_density(jax.random.fold_in(keys[2], 71), 0)
    pattern = draw_pattern(jax.random.fold_in(keys[2], 71), 0)
    return dict(density=density, pattern=pattern)


def expand_pattern(pattern):
    return jnp.repeat(jnp.repeat(pattern, BS, axis=0), BS, axis=1) > 0


def masked_product(left, right, occupied):
    full = jnp.dot(left, right, precision=lax.Precision.HIGHEST, preferred_element_type=jnp.float32)
    return jnp.where(occupied, full, jnp.zeros_like(full))


def reference(density, pattern):
    occupied = expand_pattern(pattern)
    current = density
    trace_list = []
    for iteration in range(STEPS):
        square = masked_product(current, current, occupied)
        cube_term = masked_product(current, square, occupied)
        current = 3.0 * square - 2.0 * cube_term
        trace_list.append(jnp.trace(current))
    return current, jnp.stack(trace_list)
```

```python
import jax
import jax.numpy as jnp
from jax import lax
from jax.experimental import pallas as pl
from jax.experimental.pallas import tpu as pltpu
from jax.sharding import Mesh, PartitionSpec as P

BS = 64
STEPS = 2
AXES = ("row", "z", "core", "layer")
NR, NZ, NC, NL = 4, 8, 2, 4
STRIP = 256
HALF = 128


def shift(value, axis, by):
    size = {"row": NR, "z": NZ, "core": NC, "layer": NL}[axis]
    return lax.ppermute(value, axis, [(i, (i + by) % size) for i in range(size)])


def ring(own, axis):
    half = own.shape[0] // 2
    before = shift(own, axis, 1)
    after = shift(own, axis, -1)
    far_lo = shift(before[:half], axis, 1)
    far_hi = shift(after[half:], axis, -1)
    return own, before, after, far_lo, far_hi


def plane_gather(own, first, second):
    line = ring(own, first)
    stacked = jnp.concatenate(line, axis=0).reshape(4, HALF, STRIP)
    return ring(stacked, second)


def split(value):
    hi = value.astype(jnp.bfloat16)
    lo = (value - hi.astype(jnp.float32)).astype(jnp.bfloat16)
    return hi, lo


OFFSETS = (0, 3, 1, 2)


def product_kernel(place_ref, a_ref, *refs):
    b_refs, (keep_ref, send_ref, hi_ref, lo_ref) = refs[:10], refs[10:]
    row, layer = place_ref[0], place_ref[1]

    def put(value, half, row_offset, layer_offset):
        strip = lax.rem(row + row_offset, NR) * NL + lax.rem(layer + layer_offset, NL)
        hi, lo = split(value)
        start = pl.multiple_of(strip * HALF, HALF)
        columns = pl.ds(half * STRIP, STRIP)
        hi_ref[pl.ds(start, HALF), columns] = hi
        lo_ref[pl.ds(start, HALF), columns] = lo

    for half in range(2):
        group = b_refs[5 * half : 5 * half + 5]
        for outer in range(4):
            for inner in range(4):
                if outer < 3:
                    value = group[outer][inner]
                else:
                    value = group[3 + inner // 2][inner % 2]
                if half == 0:
                    put(value, 0, OFFSETS[outer], OFFSETS[inner])
                else:
                    put(value, 1, OFFSETS[inner], OFFSETS[outer])
    total = jnp.zeros((STRIP, 2 * STRIP), jnp.float32)
    for part in range(NZ):
        hi, lo = split(a_ref[part])
        rows = pl.ds(part * STRIP, STRIP)
        b_hi, b_lo = hi_ref[rows, :], lo_ref[rows, :]
        total += jnp.dot(hi, b_hi, preferred_element_type=jnp.float32)
        total += jnp.dot(hi, b_lo, preferred_element_type=jnp.float32)
        total += jnp.dot(lo, b_hi, preferred_element_type=jnp.float32)
    keep_ref[...] = total[:HALF]
    send_ref[...] = total[HALF:]


def product(place, a_strip, b_parts):
    tile = jax.ShapeDtypeStruct((HALF, 2 * STRIP), jnp.float32)
    vmem = pl.BlockSpec(memory_space=pltpu.VMEM)
    return pl.pallas_call(
        product_kernel,
        out_shape=(tile, tile),
        in_specs=[pl.BlockSpec(memory_space=pltpu.SMEM)] + [vmem] * 11,
        out_specs=(vmem, vmem),
        scratch_shapes=[pltpu.VMEM((NR * NL * HALF, 2 * STRIP), jnp.bfloat16)] * 2,
        compiler_params=pltpu.CompilerParams(vmem_limit_bytes=32 * 1024 * 1024),
        cost_estimate=pl.CostEstimate(
            flops=6 * STRIP * 2048 * 512, bytes_accessed=7 * 1024 * 1024, transcendentals=0
        ),
    )(place, a_strip, *b_parts)


def swap(value):
    return shift(value, "core", 1)


def small_sum(value):
    value = value + swap(value)
    for axis in ("layer", "row", "z"):
        value = value + shift(value, axis, 1) + shift(value, axis, 2) + shift(value, axis, 3)
    return value + shift(value, "z", 4)


def body(density, pattern):
    row, z = lax.axis_index("row"), lax.axis_index("z")
    core, layer = lax.axis_index("core"), lax.axis_index("layer")
    place = jnp.stack([row, layer]).astype(jnp.int32)
    first_core = core == 0
    strip_row = (row * NL + layer) * STRIP + core * HALF
    row_ids = strip_row + jnp.arange(HALF, dtype=jnp.int32)
    col_ids = z * 2 * STRIP + jnp.arange(2 * STRIP, dtype=jnp.int32)
    blocks = jnp.arange(pattern.shape[0], dtype=jnp.int32)
    row_onehot = (row_ids[:, None] // BS == blocks[None, :]).astype(jnp.bfloat16)
    col_onehot = (blocks[:, None] == col_ids[None, :] // BS).astype(jnp.bfloat16)
    row_pattern = jnp.dot(
        row_onehot, pattern.astype(jnp.bfloat16), preferred_element_type=jnp.float32
    )
    occupied = (
        jnp.dot(row_pattern.astype(jnp.bfloat16), col_onehot, preferred_element_type=jnp.float32)
        > 0.5
    )
    on_diag = row_ids[:, None] == col_ids[None, :]

    own = lax.dynamic_slice_in_dim(density, layer * STRIP, STRIP, 0)
    halves = own.reshape(2, HALF, STRIP)
    b_mine = jnp.where(first_core, halves[0], halves[1])
    b_other = swap(jnp.where(first_core, halves[1], halves[0]))
    b_even = jnp.where(first_core, b_mine, b_other)
    b_odd = jnp.where(first_core, b_other, b_mine)
    left, right = own[:, :HALF], own[:, HALF:]
    a_mine = jnp.where(first_core, left, right)
    a_other = swap(jnp.where(first_core, right, left))
    a_tile = jnp.concatenate(
        [jnp.where(first_core, a_mine, a_other), jnp.where(first_core, a_other, a_mine)], axis=1
    )
    a_tile = jnp.where(
        first_core, a_tile, jnp.concatenate([a_tile[HALF:], a_tile[:HALF]], axis=0)
    )
    trace_list = []
    for iteration in range(STEPS):
        a_strip = lax.all_gather(a_tile, "z", axis=0, tiled=False)
        b_parts = plane_gather(b_even, "layer", "row") + plane_gather(b_odd, "row", "layer")
        keep, send = product(place, a_strip, b_parts)
        total = keep + swap(send)
        square = jnp.where(occupied, total, jnp.zeros_like(total))
        s_parts = plane_gather(square[:, :STRIP], "layer", "row") + plane_gather(
            square[:, STRIP:], "row", "layer"
        )
        keep, send = product(place, a_strip, s_parts)
        total = keep + swap(send)
        cube_term = jnp.where(occupied, total, jnp.zeros_like(total))
        current = 3.0 * square - 2.0 * cube_term
        diag_part = jnp.sum(jnp.where(on_diag, current, jnp.zeros_like(current)))
        trace_list.append(small_sum(jnp.full((8, 128), diag_part, jnp.float32)))
        b_even, b_odd = current[:, :STRIP], current[:, STRIP:]
        if iteration < STEPS - 1:
            low = jnp.concatenate([b_even[:, :HALF], b_odd[:, :HALF]], axis=1)
            high = jnp.concatenate([b_even[:, HALF:], b_odd[:, HALF:]], axis=1)
            mine = jnp.where(first_core, low, high)
            other = swap(jnp.where(first_core, high, low))
            a_tile = jnp.concatenate([mine, other], axis=0)
    mine = jnp.where(first_core, b_even, b_odd)
    other = swap(jnp.where(first_core, b_odd, b_even))
    tile = jnp.concatenate(
        [jnp.where(first_core, mine, other), jnp.where(first_core, other, mine)], axis=0
    )
    own, before, after, far_lo, far_hi = ring(tile, "layer")
    far = jnp.concatenate([far_lo, far_hi], axis=0)
    stacked = jnp.stack([own, after, far, before])
    purified = jnp.take(stacked, lax.rem(jnp.arange(NL) - layer + NL, NL), axis=0)
    traces = jnp.stack([t[0, 0] for t in trace_list])
    return purified.reshape(NL * STRIP, STRIP), traces


def solution(mesh):
    fine = Mesh(mesh.devices.reshape(NR, NZ, NC, NL), AXES)
    placed = P("row", ("z", "core"))
    return jax.shard_map(
        body, mesh=fine, in_specs=(placed, P()), out_specs=(placed, P()), check_vma=False
    )
```

```python
import functools

import jax
import jax.numpy as jnp
from jax import lax
from jax.experimental import pallas as pl
from jax.experimental.pallas import tpu as pltpu
from jax.sharding import Mesh, PartitionSpec as P

BS = 64
STEPS = 2
AXES = ("row", "z", "core", "layer")
NR, NZ, NC, NL = 4, 8, 2, 4
STRIP = 256
HALF = 128
WIDE = 512


def route(value, step):
    pairs = []
    for r in range(NR):
        for z in range(NZ):
            for c in range(NC):
                for l in range(NL):
                    tr, tz, tc, tl = step(r, z, c, l)
                    target = (((tr % NR) * NZ + tz % NZ) * NC + tc) * NL + tl % NL
                    pairs.append((((r * NZ + z) * NC + c) * NL + l, target))
    return lax.ppermute(value, AXES, pairs)


def first_shift(value, by):
    return route(value, lambda r, z, c, l: (r + by * c, z, c, l + by * (1 - c)))


def second_shift(value, by):
    return route(value, lambda r, z, c, l: (r + by * (1 - c), z, c, l + by * c))


def z_shift(value, by):
    return route(value, lambda r, z, c, l: (r, z + by, c, l))


def swap(value):
    return route(value, lambda r, z, c, l: (r, z, 1 - c, l))


RING = (0, -1, 1, 2)
Z_OFFSETS = (0, -1, 1, -2, 2, -3, 3, 4)


def line_gather(low, high, shift):
    low_before, low_after = shift(low, 1), shift(low, -1)
    high_before, high_after = shift(high, 1), shift(high, -1)
    low_far, high_far = shift(low_before, 1), shift(high_after, -1)
    return low, high, low_before, high_before, low_after, high_after, low_far, high_far


def plane_gather(own):
    before, after, far = (first_shift(own, -place) for place in RING[1:])
    return line_gather(jnp.stack([own, before]), jnp.stack([after, far]), second_shift)


def row_gather(stacked):
    def shift(value, by):
        return route(value, lambda r, z, c, l: (r + by, z, c, l))

    before, after = shift(stacked, 1), shift(stacked, -1)
    return stacked, before, after, shift(before[:2], 1), shift(after[2:], -1)


def z_gather(own):
    before, after = z_shift(own, 1), z_shift(own, -1)
    before2, after2 = z_shift(before, 1), z_shift(after, -1)
    before3, after3 = z_shift(before2, 1), z_shift(after2, -1)
    first_core = lax.axis_index("core") == 0
    far = route(
        jnp.where(first_core, before3, after3),
        lambda r, z, c, l: (r, z + 1 - 2 * c, c, l),
    )
    return own, before, after, before2, after2, before3, after3, far


def split(value):
    hi = value.astype(jnp.bfloat16)
    lo = (value - hi.astype(jnp.float32)).astype(jnp.bfloat16)
    return hi, lo


def product_kernel(by_row, place_ref, *refs):
    b_count = 5 if by_row else 8
    a_refs, b_refs = refs[: -6 - b_count], refs[-6 - b_count : -6]
    keep_ref, send_ref, a_all, b_all, a_sem, b_sem = refs[-6:]
    row, z, core, layer = (place_ref[i] for i in range(4))
    a_copies = []
    if len(a_refs) == 1:
        a_copies.append(pltpu.make_async_copy(a_refs[0], a_all, a_sem.at[0]))
        a_copies[-1].start()
    else:
        for i, offset in enumerate(Z_OFFSETS):
            at = lax.rem(z + offset + NZ, NZ)
            a_copies.append(
                pltpu.make_async_copy(a_refs[i], a_all.at[pl.ds(2 * at, 2)], a_sem.at[i])
            )
            a_copies[-1].start()
    b_copies = []
    for i in range(8):
        if not by_row:
            ref = b_refs[i]
        else:
            ref = b_refs[i // 2].at[pl.ds(2 * (i % 2), 2)] if i < 6 else b_refs[i - 3]
        b_copies.append(pltpu.make_async_copy(ref, b_all.at[i], b_sem.at[i]))
        b_copies[-1].start()
    for copy in a_copies:
        copy.wait()
    total = jnp.zeros((STRIP, WIDE), jnp.float32)
    for i in range(8):
        second = RING[i // 2]
        b_copies[i].wait()
        a_parts = []
        for slot in (2 * (i % 2), 2 * (i % 2) + 1):
            if by_row:
                strip = lax.rem(row + second + NR, NR) * NL + slot
            else:
                first = RING[slot]
                row_offset = jnp.where(core == 0, second, first)
                layer_offset = jnp.where(core == 0, first, second)
                strip = lax.rem(row + row_offset + NR, NR) * NL + lax.rem(
                    layer + layer_offset + NL, NL
                )
            a_parts.append(a_all[strip])
        a_hi, a_lo = split(jnp.concatenate(a_parts, axis=1))
        b_hi, b_lo = split(b_all[i].reshape(STRIP, WIDE))
        total += jnp.dot(
            jnp.concatenate([a_hi, a_hi, a_lo], axis=1),
            jnp.concatenate([b_hi, b_lo, b_hi], axis=0),
            preferred_element_type=jnp.float32,
        )
    keep_ref[...] = total[:HALF]
    send_ref[...] = total[HALF:]


def product(place, a_parts, b_parts, by_row=False):
    tile = jax.ShapeDtypeStruct((HALF, WIDE), jnp.float32)
    anywhere = pl.BlockSpec(memory_space=pl.ANY)
    vmem = pl.BlockSpec(memory_space=pltpu.VMEM)
    return pl.pallas_call(
        functools.partial(product_kernel, by_row),
        out_shape=(tile, tile),
        in_specs=[pl.BlockSpec(memory_space=pltpu.SMEM)] + [anywhere] * (len(a_parts) + len(b_parts)),
        out_specs=(vmem, vmem),
        scratch_shapes=[
            pltpu.VMEM((2 * NZ, STRIP, HALF), jnp.float32),
            pltpu.VMEM((8, 2, HALF, WIDE), jnp.float32),
            pltpu.SemaphoreType.DMA((8,)),
            pltpu.SemaphoreType.DMA((8,)),
        ],
        compiler_params=pltpu.CompilerParams(vmem_limit_bytes=48 * 1024 * 1024),
        cost_estimate=pl.CostEstimate(
            flops=6 * STRIP * 2048 * WIDE, bytes_accessed=7 * 1024 * 1024, transcendentals=0
        ),
    )(place, *a_parts, *b_parts)


def sum_over_chips(parts):
    mine = jnp.broadcast_to(parts, (NR * NZ * NL, HALF))
    theirs = lax.all_to_all(mine, ("row", "z", "layer"), 0, 0, tiled=True)
    return jnp.sum(theirs, axis=0)[:STEPS]


def body(density, pattern):
    row, z = lax.axis_index("row"), lax.axis_index("z")
    core, layer = lax.axis_index("core"), lax.axis_index("layer")
    place = jnp.stack([row, z, core, layer]).astype(jnp.int32)
    first_core = core == 0
    strip_row = (row * NL + layer) * STRIP + core * HALF
    row_ids = strip_row + jnp.arange(HALF, dtype=jnp.int32)
    col_ids = z * WIDE + jnp.arange(WIDE, dtype=jnp.int32)
    blocks = jnp.arange(pattern.shape[0], dtype=jnp.int32)
    row_onehot = (row_ids[:, None] // BS == blocks[None, :]).astype(jnp.bfloat16)
    col_onehot = (blocks[:, None] == col_ids[None, :] // BS).astype(jnp.bfloat16)
    row_pattern = jnp.dot(
        row_onehot, pattern.astype(jnp.bfloat16), preferred_element_type=jnp.float32
    )
    occupied = (
        jnp.dot(row_pattern.astype(jnp.bfloat16), col_onehot, preferred_element_type=jnp.float32)
        > 0.5
    )
    on_diag = row_ids[:, None] == col_ids[None, :]

    near = lax.dynamic_slice_in_dim(density, layer * STRIP + core * HALF, HALF, 0)
    away = lax.dynamic_slice_in_dim(density, layer * STRIP + (1 - core) * HALF, HALF, 0)
    give = jnp.where(
        first_core,
        jnp.concatenate([away[:, HALF:], near[:, HALF:]], axis=0),
        jnp.concatenate([away[:, :HALF], near[:, :HALF]], axis=0),
    )
    a_mine = jnp.where(
        first_core,
        jnp.concatenate([near[:, :HALF], away[:, :HALF]], axis=0),
        jnp.concatenate([near[:, HALF:], away[:, HALF:]], axis=0),
    )
    a_other = swap(give)
    a_tile = jnp.where(
        first_core, jnp.stack([a_mine, a_other]), jnp.stack([a_other, a_mine])
    )
    density, a_tile = lax.optimization_barrier((density, a_tile))
    strips = density.reshape(NL, 2, HALF, STRIP)
    near = jnp.where(first_core, strips[:, 0], strips[:, 1])
    away = jnp.where(first_core, strips[:, 1], strips[:, 0])
    others = swap(away)
    b_tiles = jnp.where(
        first_core,
        jnp.concatenate([near, others], axis=2),
        jnp.concatenate([others, near], axis=2),
    )
    def diagonal(tile):
        return jnp.sum(jnp.where(on_diag, tile, jnp.zeros_like(tile)))

    a_parts = z_gather(a_tile)
    keep, send = product(place, a_parts, row_gather(b_tiles), by_row=True)
    total = keep + swap(send)
    square = jnp.where(occupied, total, jnp.zeros_like(total))
    keep, send = product(place, a_parts, plane_gather(square))
    total = keep + swap(send)
    cube_term = jnp.where(occupied, total, jnp.zeros_like(total))
    current = 3.0 * square - 2.0 * cube_term
    first_trace = diagonal(current)

    quarters = current.reshape(HALF, 4, HALF)
    low = jnp.stack([quarters[:, 0], quarters[:, 2]])
    high = jnp.stack([quarters[:, 1], quarters[:, 3]])
    mine = jnp.where(first_core, low, high)
    other = swap(jnp.where(first_core, high, low))
    a_tile = jnp.concatenate([mine, other], axis=1)
    a_tile, b_tile = lax.optimization_barrier((a_tile, current))
    a_parts = (lax.all_gather(a_tile, "z", axis=0, tiled=True),)
    b_parts = plane_gather(b_tile)
    keep, send = product(place, a_parts, b_parts)
    total = keep + swap(send)
    square = jnp.where(occupied, total, jnp.zeros_like(total))
    s_parts = plane_gather(square)
    keep, send = product(place, a_parts, s_parts)
    total = keep + swap(send)
    cube_term = jnp.where(occupied, total, jnp.zeros_like(total))
    current = 3.0 * square - 2.0 * cube_term

    lanes = lax.broadcasted_iota(jnp.int32, (8, STRIP), 1)
    parts = jnp.where(lanes == 0, first_trace, diagonal(current))
    even, odd = current[:, :STRIP], current[:, STRIP:]
    mine = jnp.where(first_core, even, odd)
    other = swap(jnp.concatenate([jnp.where(first_core, odd, even), parts], axis=0))
    traces = sum_over_chips(parts[0, :HALF] + other[HALF, :HALF])
    other = other[:HALF]
    tile = jnp.where(first_core, jnp.stack([mine, other]), jnp.stack([other, mine]))
    before = route(tile, lambda r, z, c, l: (r, z, c, l + 1))
    after = route(tile, lambda r, z, c, l: (r, z, c, l - 1))
    far = route(
        jnp.where(first_core, before, after),
        lambda r, z, c, l: (r, z, c, l + 1 - 2 * c),
    )
    stacked = jnp.stack([tile, after, far, before])
    purified = jnp.take(stacked, lax.rem(jnp.arange(NL) - layer + NL, NL), axis=0)
    return purified.reshape(NL * STRIP, STRIP), traces


def solution(mesh):
    fine = Mesh(mesh.devices.reshape(NR, NZ, NC, NL), AXES)
    placed = P("row", ("z", "core"))
    return jax.shard_map(
        body, mesh=fine, in_specs=(placed, P()), out_specs=(placed, P()), check_vma=False
    )
```

```python
import functools

import jax
import jax.numpy as jnp
from jax import lax
from jax.experimental import pallas as pl
from jax.experimental.pallas import tpu as pltpu
from jax.sharding import Mesh, PartitionSpec as P

BS = 64
STEPS = 2
AXES = ("row", "z", "core", "layer")
NR, NZ, NC, NL = 4, 8, 2, 4
STRIP = 256
HALF = 128
WIDE = 512


def route(value, step):
    pairs = []
    for r in range(NR):
        for z in range(NZ):
            for c in range(NC):
                for l in range(NL):
                    tr, tz, tc, tl = step(r, z, c, l)
                    target = (((tr % NR) * NZ + tz % NZ) * NC + tc) * NL + tl % NL
                    pairs.append((((r * NZ + z) * NC + c) * NL + l, target))
    return lax.ppermute(value, AXES, pairs)


def first_shift(value, by):
    return route(value, lambda r, z, c, l: (r + by * c, z, c, l + by * (1 - c)))


def second_shift(value, by):
    return route(value, lambda r, z, c, l: (r + by * (1 - c), z, c, l + by * c))


def z_shift(value, by):
    return route(value, lambda r, z, c, l: (r, z + by, c, l))


def swap(value):
    return route(value, lambda r, z, c, l: (r, z, 1 - c, l))


RING = (0, -1, 1, 2)
Z_OFFSETS = (0, -1, 1, -2, 2, -3, 3, 4)


def line_gather(low, high, shift):
    low_before, low_after = shift(low, 1), shift(low, -1)
    high_before, high_after = shift(high, 1), shift(high, -1)
    low_far, high_far = shift(low_before, 1), shift(high_after, -1)
    return low, high, low_before, high_before, low_after, high_after, low_far, high_far


def plane_gather(own):
    before, after = first_shift(own, 1), first_shift(own, -1)
    late, before = lax.optimization_barrier((own, before))
    far = first_shift(late, 2)
    return line_gather(jnp.stack([own, before]), jnp.stack([after, far]), second_shift)


def row_gather(stacked):
    def shift(value, by):
        return route(value, lambda r, z, c, l: (r + by, z, c, l))

    before, after = shift(stacked, 1), shift(stacked, -1)
    return stacked, before, after, shift(before[:2], 1), shift(after[2:], -1)


def z_gather(own):
    before, after = z_shift(own, 1), z_shift(own, -1)
    before2, after2 = z_shift(before, 1), z_shift(after, -1)
    before3, after3 = z_shift(before2, 1), z_shift(after2, -1)
    first_core = lax.axis_index("core") == 0
    far = route(
        jnp.where(first_core, before3, after3),
        lambda r, z, c, l: (r, z + 1 - 2 * c, c, l),
    )
    return own, before, after, before2, after2, before3, after3, far


def split(value):
    hi = value.astype(jnp.bfloat16)
    lo = (value - hi.astype(jnp.float32)).astype(jnp.bfloat16)
    return hi, lo


def product_kernel(by_row, place_ref, *refs):
    b_count = 5 if by_row else 8
    a_refs, b_refs = refs[: -6 - b_count], refs[-6 - b_count : -6]
    keep_ref, send_ref, a_all, b_all, a_sem, b_sem = refs[-6:]
    row, z, core, layer = (place_ref[i] for i in range(4))
    a_copies = []
    if len(a_refs) == 1:
        a_copies.append(pltpu.make_async_copy(a_refs[0], a_all, a_sem.at[0]))
        a_copies[-1].start()
    else:
        for i, offset in enumerate(Z_OFFSETS):
            at = lax.rem(z + offset + NZ, NZ)
            a_copies.append(
                pltpu.make_async_copy(a_refs[i], a_all.at[pl.ds(2 * at, 2)], a_sem.at[i])
            )
            a_copies[-1].start()
    b_copies = []
    for i in range(8):
        if not by_row:
            ref = b_refs[i]
        else:
            ref = b_refs[i // 2].at[pl.ds(2 * (i % 2), 2)] if i < 6 else b_refs[i - 3]
        b_copies.append(pltpu.make_async_copy(ref, b_all.at[i], b_sem.at[i]))
        b_copies[-1].start()
    for copy in a_copies:
        copy.wait()
    total = jnp.zeros((STRIP, WIDE), jnp.float32)
    for i in range(8):
        second = RING[i // 2]
        b_copies[i].wait()
        a_parts = []
        for slot in (2 * (i % 2), 2 * (i % 2) + 1):
            if by_row:
                strip = lax.rem(row + second + NR, NR) * NL + slot
            else:
                first = RING[slot]
                row_offset = jnp.where(core == 0, second, first)
                layer_offset = jnp.where(core == 0, first, second)
                strip = lax.rem(row + row_offset + NR, NR) * NL + lax.rem(
                    layer + layer_offset + NL, NL
                )
            a_parts.append(a_all[strip])
        a_hi, a_lo = split(jnp.concatenate(a_parts, axis=1))
        b_hi, b_lo = split(b_all[i].reshape(STRIP, WIDE))
        total += jnp.dot(
            jnp.concatenate([a_hi, a_hi, a_lo], axis=1),
            jnp.concatenate([b_hi, b_lo, b_hi], axis=0),
            preferred_element_type=jnp.float32,
        )
    keep_ref[...] = total[:HALF]
    send_ref[...] = total[HALF:]


def product(place, a_parts, b_parts, by_row=False):
    tile = jax.ShapeDtypeStruct((HALF, WIDE), jnp.float32)
    anywhere = pl.BlockSpec(memory_space=pl.ANY)
    vmem = pl.BlockSpec(memory_space=pltpu.VMEM)
    return pl.pallas_call(
        functools.partial(product_kernel, by_row),
        out_shape=(tile, tile),
        in_specs=[pl.BlockSpec(memory_space=pltpu.SMEM)] + [anywhere] * (len(a_parts) + len(b_parts)),
        out_specs=(vmem, vmem),
        scratch_shapes=[
            pltpu.VMEM((2 * NZ, STRIP, HALF), jnp.float32),
            pltpu.VMEM((8, 2, HALF, WIDE), jnp.float32),
            pltpu.SemaphoreType.DMA((8,)),
            pltpu.SemaphoreType.DMA((8,)),
        ],
        compiler_params=pltpu.CompilerParams(vmem_limit_bytes=48 * 1024 * 1024),
        cost_estimate=pl.CostEstimate(
            flops=6 * STRIP * 2048 * WIDE, bytes_accessed=7 * 1024 * 1024, transcendentals=0
        ),
    )(place, *a_parts, *b_parts)


def sum_everywhere(first, second):
    lanes = lax.broadcasted_iota(jnp.int32, (NR * NZ * NC * NL, HALF), 1)
    mine = jnp.where(lanes == 0, first, second)
    theirs = lax.all_to_all(mine, AXES, 0, 0, tiled=True)
    return jnp.sum(theirs, axis=0)[:STEPS]


def body(density, pattern):
    row, z = lax.axis_index("row"), lax.axis_index("z")
    core, layer = lax.axis_index("core"), lax.axis_index("layer")
    place = jnp.stack([row, z, core, layer]).astype(jnp.int32)
    first_core = core == 0
    strip_row = (row * NL + layer) * STRIP + core * HALF
    row_ids = strip_row + jnp.arange(HALF, dtype=jnp.int32)
    col_ids = z * WIDE + jnp.arange(WIDE, dtype=jnp.int32)
    blocks = jnp.arange(pattern.shape[0], dtype=jnp.int32)
    row_onehot = (row_ids[:, None] // BS == blocks[None, :]).astype(jnp.bfloat16)
    col_onehot = (blocks[:, None] == col_ids[None, :] // BS).astype(jnp.bfloat16)
    row_pattern = jnp.dot(
        row_onehot, pattern.astype(jnp.bfloat16), preferred_element_type=jnp.float32
    )
    occupied = (
        jnp.dot(row_pattern.astype(jnp.bfloat16), col_onehot, preferred_element_type=jnp.float32)
        > 0.5
    )
    on_diag = row_ids[:, None] == col_ids[None, :]

    near = lax.dynamic_slice_in_dim(density, layer * STRIP + core * HALF, HALF, 0)
    away = lax.dynamic_slice_in_dim(density, layer * STRIP + (1 - core) * HALF, HALF, 0)
    give = jnp.where(
        first_core,
        jnp.concatenate([away[:, HALF:], near[:, HALF:]], axis=0),
        jnp.concatenate([away[:, :HALF], near[:, :HALF]], axis=0),
    )
    a_mine = jnp.where(
        first_core,
        jnp.concatenate([near[:, :HALF], away[:, :HALF]], axis=0),
        jnp.concatenate([near[:, HALF:], away[:, HALF:]], axis=0),
    )
    a_other = swap(give)
    a_tile = jnp.where(
        first_core, jnp.stack([a_mine, a_other]), jnp.stack([a_other, a_mine])
    )
    density, a_tile = lax.optimization_barrier((density, a_tile))
    strips = density.reshape(NL, 2, HALF, STRIP)
    near = jnp.where(first_core, strips[:, 0], strips[:, 1])
    away = jnp.where(first_core, strips[:, 1], strips[:, 0])
    others = swap(away)
    b_tiles = jnp.where(
        first_core,
        jnp.concatenate([near, others], axis=2),
        jnp.concatenate([others, near], axis=2),
    )
    def diagonal(tile):
        return jnp.sum(jnp.where(on_diag, tile, jnp.zeros_like(tile)))

    a_parts = z_gather(a_tile)
    keep, send = product(place, a_parts, row_gather(b_tiles), by_row=True)
    total = keep + swap(send)
    square = jnp.where(occupied, total, jnp.zeros_like(total))
    keep, send = product(place, a_parts, plane_gather(square))
    total = keep + swap(send)
    cube_term = jnp.where(occupied, total, jnp.zeros_like(total))
    current = 3.0 * square - 2.0 * cube_term
    first_trace = diagonal(current)

    quarters = current.reshape(HALF, 4, HALF)
    low = jnp.stack([quarters[:, 0], quarters[:, 2]])
    high = jnp.stack([quarters[:, 1], quarters[:, 3]])
    mine = jnp.where(first_core, low, high)
    other = swap(jnp.where(first_core, high, low))
    a_tile = jnp.concatenate([mine, other], axis=1)
    a_tile, b_tile = lax.optimization_barrier((a_tile, current))
    a_parts = (lax.all_gather(a_tile, "z", axis=0, tiled=True),)
    b_parts = plane_gather(b_tile)
    keep, send = product(place, a_parts, b_parts)
    total = keep + swap(send)
    square = jnp.where(occupied, total, jnp.zeros_like(total))
    s_parts = plane_gather(square)
    keep, send = product(place, a_parts, s_parts)
    total = keep + swap(send)
    cube_term = jnp.where(occupied, total, jnp.zeros_like(total))
    current = 3.0 * square - 2.0 * cube_term

    traces = sum_everywhere(first_trace, diagonal(current))
    even, odd = current[:, :STRIP], current[:, STRIP:]
    mine = jnp.where(first_core, even, odd)
    other = swap(jnp.where(first_core, odd, even))
    tile = jnp.where(first_core, jnp.stack([mine, other]), jnp.stack([other, mine]))
    before = route(tile, lambda r, z, c, l: (r, z, c, l + 1))
    after = route(tile, lambda r, z, c, l: (r, z, c, l - 1))
    far = route(
        jnp.where(first_core, before, after),
        lambda r, z, c, l: (r, z, c, l + 1 - 2 * c),
    )
    stacked = jnp.stack([tile, after, far, before])
    purified = jnp.take(stacked, lax.rem(jnp.arange(NL) - layer + NL, NL), axis=0)
    return purified.reshape(NL * STRIP, STRIP), traces


def solution(mesh):
    fine = Mesh(mesh.devices.reshape(NR, NZ, NC, NL), AXES)
    placed = P("row", ("z", "core"))
    return jax.shard_map(
        body, mesh=fine, in_specs=(placed, P()), out_specs=(placed, P()), check_vma=False
    )
```

```python
import functools

import jax
import jax.numpy as jnp
from jax import lax
from jax.experimental import pallas as pl
from jax.experimental.pallas import tpu as pltpu
from jax.sharding import Mesh, PartitionSpec as P

BS = 64
STEPS = 2
AXES = ("row", "z", "core", "layer")
NR, NZ, NC, NL = 4, 8, 2, 4
STRIP = 256
HALF = 128
WIDE = 512


def route(value, step):
    pairs = []
    for r in range(NR):
        for z in range(NZ):
            for c in range(NC):
                for l in range(NL):
                    tr, tz, tc, tl = step(r, z, c, l)
                    target = (((tr % NR) * NZ + tz % NZ) * NC + tc) * NL + tl % NL
                    pairs.append((((r * NZ + z) * NC + c) * NL + l, target))
    return lax.ppermute(value, AXES, pairs)


def first_shift(value, by):
    return route(value, lambda r, z, c, l: (r + by * c, z, c, l + by * (1 - c)))


def second_shift(value, by):
    return route(value, lambda r, z, c, l: (r + by * (1 - c), z, c, l + by * c))


def z_shift(value, by):
    return route(value, lambda r, z, c, l: (r, z + by, c, l))


def swap(value):
    return route(value, lambda r, z, c, l: (r, z, 1 - c, l))


RING = (0, -1, 1, 2)
Z_OFFSETS = (0, -1, 1, -2, 2, -3, 3, 4)


def line_gather(low, high, shift):
    low_before, low_after = shift(low, 1), shift(low, -1)
    high_before, high_after = shift(high, 1), shift(high, -1)
    low_far, high_far = shift(low_before, 1), shift(high_after, -1)
    return low, high, low_before, high_before, low_after, high_after, low_far, high_far


def plane_gather(own):
    before, after, far = (first_shift(own, -place) for place in RING[1:])
    return line_gather(jnp.stack([own, before]), jnp.stack([after, far]), second_shift)


def row_gather(stacked):
    def shift(value, by):
        return route(value, lambda r, z, c, l: (r + by, z, c, l))

    before, after = shift(stacked, 1), shift(stacked, -1)
    return stacked, before, after, shift(before[:2], 1), shift(after[2:], -1)


def z_gather(own):
    before, after = z_shift(own, 1), z_shift(own, -1)
    before2, after2 = z_shift(before, 1), z_shift(after, -1)
    before3, after3 = z_shift(before2, 1), z_shift(after2, -1)
    first_core = lax.axis_index("core") == 0
    far = route(
        jnp.where(first_core, before3, after3),
        lambda r, z, c, l: (r, z + 1 - 2 * c, c, l),
    )
    return own, before, after, before2, after2, before3, after3, far


def split(value):
    hi = value.astype(jnp.bfloat16)
    lo = (value - hi.astype(jnp.float32)).astype(jnp.bfloat16)
    return hi, lo


def product_kernel(by_row, place_ref, *refs):
    b_count = 5 if by_row else 8
    a_refs, b_refs = refs[: -6 - b_count], refs[-6 - b_count : -6]
    keep_ref, send_ref, a_all, b_all, a_sem, b_sem = refs[-6:]
    row, z, core, layer = (place_ref[i] for i in range(4))
    a_copies = []
    if len(a_refs) == 1:
        a_copies.append(pltpu.make_async_copy(a_refs[0], a_all, a_sem.at[0]))
        a_copies[-1].start()
    else:
        for i, offset in enumerate(Z_OFFSETS):
            at = lax.rem(z + offset + NZ, NZ)
            a_copies.append(
                pltpu.make_async_copy(a_refs[i], a_all.at[pl.ds(2 * at, 2)], a_sem.at[i])
            )
            a_copies[-1].start()
    b_copies = []
    for i in range(8):
        if not by_row:
            ref = b_refs[i]
        else:
            ref = b_refs[i // 2].at[pl.ds(2 * (i % 2), 2)] if i < 6 else b_refs[i - 3]
        b_copies.append(pltpu.make_async_copy(ref, b_all.at[i], b_sem.at[i]))
        b_copies[-1].start()
    for copy in a_copies:
        copy.wait()
    total = jnp.zeros((STRIP, WIDE), jnp.float32)
    for i in range(8):
        second = RING[i // 2]
        b_copies[i].wait()
        a_parts = []
        for slot in (2 * (i % 2), 2 * (i % 2) + 1):
            if by_row:
                strip = lax.rem(row + second + NR, NR) * NL + slot
            else:
                first = RING[slot]
                row_offset = jnp.where(core == 0, second, first)
                layer_offset = jnp.where(core == 0, first, second)
                strip = lax.rem(row + row_offset + NR, NR) * NL + lax.rem(
                    layer + layer_offset + NL, NL
                )
            a_parts.append(a_all[strip])
        a_hi, a_lo = split(jnp.concatenate(a_parts, axis=1))
        b_hi, b_lo = split(b_all[i].reshape(STRIP, WIDE))
        total += jnp.dot(
            jnp.concatenate([a_hi, a_hi, a_lo], axis=1),
            jnp.concatenate([b_hi, b_lo, b_hi], axis=0),
            preferred_element_type=jnp.float32,
        )
    keep_ref[...] = total[:HALF]
    send_ref[...] = total[HALF:]


def product(place, a_parts, b_parts, by_row=False):
    tile = jax.ShapeDtypeStruct((HALF, WIDE), jnp.float32)
    anywhere = pl.BlockSpec(memory_space=pl.ANY)
    vmem = pl.BlockSpec(memory_space=pltpu.VMEM)
    return pl.pallas_call(
        functools.partial(product_kernel, by_row),
        out_shape=(tile, tile),
        in_specs=[pl.BlockSpec(memory_space=pltpu.SMEM)] + [anywhere] * (len(a_parts) + len(b_parts)),
        out_specs=(vmem, vmem),
        scratch_shapes=[
            pltpu.VMEM((2 * NZ, STRIP, HALF), jnp.float32),
            pltpu.VMEM((8, 2, HALF, WIDE), jnp.float32),
            pltpu.SemaphoreType.DMA((8,)),
            pltpu.SemaphoreType.DMA((8,)),
        ],
        compiler_params=pltpu.CompilerParams(vmem_limit_bytes=48 * 1024 * 1024),
        cost_estimate=pl.CostEstimate(
            flops=6 * STRIP * 2048 * WIDE, bytes_accessed=7 * 1024 * 1024, transcendentals=0
        ),
    )(place, *a_parts, *b_parts)


def sum_everywhere(first, second):
    parts = jnp.where(jnp.arange(HALF) == 0, first, second)
    mine = jnp.broadcast_to(parts, (NR * NZ * NC * NL, HALF))
    theirs = lax.all_to_all(mine, AXES, 0, 0, tiled=True)
    return jnp.sum(theirs, axis=0)[:STEPS]


def body(density, pattern):
    row, z = lax.axis_index("row"), lax.axis_index("z")
    core, layer = lax.axis_index("core"), lax.axis_index("layer")
    place = jnp.stack([row, z, core, layer]).astype(jnp.int32)
    first_core = core == 0
    strip_row = (row * NL + layer) * STRIP + core * HALF
    row_ids = strip_row + jnp.arange(HALF, dtype=jnp.int32)
    col_ids = z * WIDE + jnp.arange(WIDE, dtype=jnp.int32)
    blocks = jnp.arange(pattern.shape[0], dtype=jnp.int32)
    row_onehot = (row_ids[:, None] // BS == blocks[None, :]).astype(jnp.bfloat16)
    col_onehot = (blocks[:, None] == col_ids[None, :] // BS).astype(jnp.bfloat16)
    row_pattern = jnp.dot(
        row_onehot, pattern.astype(jnp.bfloat16), preferred_element_type=jnp.float32
    )
    occupied = (
        jnp.dot(row_pattern.astype(jnp.bfloat16), col_onehot, preferred_element_type=jnp.float32)
        > 0.5
    )
    on_diag = row_ids[:, None] == col_ids[None, :]

    near = lax.dynamic_slice_in_dim(density, layer * STRIP + core * HALF, HALF, 0)
    away = lax.dynamic_slice_in_dim(density, layer * STRIP + (1 - core) * HALF, HALF, 0)
    give = jnp.where(
        first_core,
        jnp.concatenate([away[:, HALF:], near[:, HALF:]], axis=0),
        jnp.concatenate([away[:, :HALF], near[:, :HALF]], axis=0),
    )
    a_mine = jnp.where(
        first_core,
        jnp.concatenate([near[:, :HALF], away[:, :HALF]], axis=0),
        jnp.concatenate([near[:, HALF:], away[:, HALF:]], axis=0),
    )
    a_other = swap(give)
    a_tile = jnp.where(
        first_core, jnp.stack([a_mine, a_other]), jnp.stack([a_other, a_mine])
    )
    a_parts = z_gather(a_tile)
    density, _ = lax.optimization_barrier((density, a_parts[1]))
    strips = density.reshape(NL, 2, HALF, STRIP)
    near = jnp.where(first_core, strips[:, 0], strips[:, 1])
    away = jnp.where(first_core, strips[:, 1], strips[:, 0])
    others = swap(away)
    b_tiles = jnp.where(
        first_core,
        jnp.concatenate([near, others], axis=2),
        jnp.concatenate([others, near], axis=2),
    )
    def diagonal(tile):
        return jnp.sum(jnp.where(on_diag, tile, jnp.zeros_like(tile)))

    keep, send = product(place, a_parts, row_gather(b_tiles), by_row=True)
    total = keep + swap(send)
    square = jnp.where(occupied, total, jnp.zeros_like(total))
    keep, send = product(place, a_parts, plane_gather(square))
    total = keep + swap(send)
    cube_term = jnp.where(occupied, total, jnp.zeros_like(total))
    current = 3.0 * square - 2.0 * cube_term
    first_trace = diagonal(current)

    quarters = current.reshape(HALF, 4, HALF)
    low = jnp.stack([quarters[:, 0], quarters[:, 2]])
    high = jnp.stack([quarters[:, 1], quarters[:, 3]])
    mine = jnp.where(first_core, low, high)
    other = swap(jnp.where(first_core, high, low))
    a_tile = jnp.concatenate([mine, other], axis=1)
    a_tile, b_tile = lax.optimization_barrier((a_tile, current))
    a_parts = (lax.all_gather(a_tile, "z", axis=0, tiled=True),)
    b_parts = plane_gather(b_tile)
    keep, send = product(place, a_parts, b_parts)
    total = keep + swap(send)
    square = jnp.where(occupied, total, jnp.zeros_like(total))
    s_parts = plane_gather(square)
    keep, send = product(place, a_parts, s_parts)
    total = keep + swap(send)
    cube_term = jnp.where(occupied, total, jnp.zeros_like(total))
    current = 3.0 * square - 2.0 * cube_term

    traces = sum_everywhere(first_trace, diagonal(current))
    even, odd = current[:, :STRIP], current[:, STRIP:]
    mine = jnp.where(first_core, even, odd)
    other = swap(jnp.where(first_core, odd, even))
    tile = jnp.where(first_core, jnp.stack([mine, other]), jnp.stack([other, mine]))
    before = route(tile, lambda r, z, c, l: (r, z, c, l + 1))
    after = route(tile, lambda r, z, c, l: (r, z, c, l - 1))
    far = route(
        jnp.where(first_core, before, after),
        lambda r, z, c, l: (r, z, c, l + 1 - 2 * c),
    )
    stacked = jnp.stack([tile, after, far, before])
    purified = jnp.take(stacked, lax.rem(jnp.arange(NL) - layer + NL, NL), axis=0)
    return purified.reshape(NL * STRIP, STRIP), traces


def solution(mesh):
    fine = Mesh(mesh.devices.reshape(NR, NZ, NC, NL), AXES)
    placed = P("row", ("z", "core"))
    return jax.shard_map(
        body, mesh=fine, in_specs=(placed, P()), out_specs=(placed, P()), check_vma=False
    )
```

```python
import functools

import jax
import jax.numpy as jnp
from jax import lax
from jax.experimental import pallas as pl
from jax.experimental.pallas import tpu as pltpu
from jax.sharding import Mesh, PartitionSpec as P

BS = 64
STEPS = 2
AXES = ("row", "z", "core", "layer")
NR, NZ, NC, NL = 4, 8, 2, 4
STRIP = 256
HALF = 128
WIDE = 512


def route(value, step):
    pairs = []
    for r in range(NR):
        for z in range(NZ):
            for c in range(NC):
                for l in range(NL):
                    tr, tz, tc, tl = step(r, z, c, l)
                    target = (((tr % NR) * NZ + tz % NZ) * NC + tc) * NL + tl % NL
                    pairs.append((((r * NZ + z) * NC + c) * NL + l, target))
    return lax.ppermute(value, AXES, pairs)


def first_shift(value, by):
    return route(value, lambda r, z, c, l: (r + by * c, z, c, l + by * (1 - c)))


def second_shift(value, by):
    return route(value, lambda r, z, c, l: (r + by * (1 - c), z, c, l + by * c))


def z_shift(value, by):
    return route(value, lambda r, z, c, l: (r, z + by, c, l))


def swap(value):
    return route(value, lambda r, z, c, l: (r, z, 1 - c, l))


RING = (0, -1, 1, 2)
Z_OFFSETS = (0, -1, 1, -2, 2, -3, 3, 4)


def line_gather(low, high, shift):
    low_before, low_after = shift(low, 1), shift(low, -1)
    high_before, high_after = shift(high, 1), shift(high, -1)
    low_far, high_far = shift(low_before, 1), shift(high_after, -1)
    return low, high, low_before, high_before, low_after, high_after, low_far, high_far


def plane_gather(own):
    before, after, far = (first_shift(own, -place) for place in RING[1:])
    return line_gather(jnp.stack([own, before]), jnp.stack([after, far]), second_shift)


def row_gather(stacked):
    def shift(value, by):
        return route(value, lambda r, z, c, l: (r + by, z, c, l))

    before, after = shift(stacked, 1), shift(stacked, -1)
    return stacked, before, after, shift(before[:2], 1), shift(after[2:], -1)


def z_gather(own):
    before, after = z_shift(own, 1), z_shift(own, -1)
    before2, after2 = z_shift(before, 1), z_shift(after, -1)
    before3, after3 = z_shift(before2, 1), z_shift(after2, -1)
    first_core = lax.axis_index("core") == 0
    far = route(
        jnp.where(first_core, before3, after3),
        lambda r, z, c, l: (r, z + 1 - 2 * c, c, l),
    )
    return own, before, after, before2, after2, before3, after3, far


def split(value):
    hi = value.astype(jnp.bfloat16)
    lo = (value - hi.astype(jnp.float32)).astype(jnp.bfloat16)
    return hi, lo


def product_kernel(by_row, place_ref, *refs):
    b_count = 5 if by_row else 8
    a_refs, b_refs = refs[: -6 - b_count], refs[-6 - b_count : -6]
    keep_ref, send_ref, a_all, b_all, a_sem, b_sem = refs[-6:]
    row, z, core, layer = (place_ref[i] for i in range(4))
    a_copies = []
    if len(a_refs) == 1:
        a_copies.append(pltpu.make_async_copy(a_refs[0], a_all, a_sem.at[0]))
        a_copies[-1].start()
    else:
        for i, offset in enumerate(Z_OFFSETS):
            at = lax.rem(z + offset + NZ, NZ)
            a_copies.append(
                pltpu.make_async_copy(a_refs[i], a_all.at[pl.ds(2 * at, 2)], a_sem.at[i])
            )
            a_copies[-1].start()
    b_copies = []
    for i in range(8):
        if not by_row:
            ref = b_refs[i]
        else:
            ref = b_refs[i // 2].at[pl.ds(2 * (i % 2), 2)] if i < 6 else b_refs[i - 3]
        b_copies.append(pltpu.make_async_copy(ref, b_all.at[i], b_sem.at[i]))
        b_copies[-1].start()
    for copy in a_copies:
        copy.wait()
    total = jnp.zeros((STRIP, WIDE), jnp.float32)
    for i in range(8):
        second = RING[i // 2]
        b_copies[i].wait()
        a_parts = []
        for slot in (2 * (i % 2), 2 * (i % 2) + 1):
            if by_row:
                strip = lax.rem(row + second + NR, NR) * NL + slot
            else:
                first = RING[slot]
                row_offset = jnp.where(core == 0, second, first)
                layer_offset = jnp.where(core == 0, first, second)
                strip = lax.rem(row + row_offset + NR, NR) * NL + lax.rem(
                    layer + layer_offset + NL, NL
                )
            a_parts.append(a_all[strip])
        a_hi, a_lo = split(jnp.concatenate(a_parts, axis=1))
        b_hi, b_lo = split(b_all[i].reshape(STRIP, WIDE))
        total += jnp.dot(
            jnp.concatenate([a_hi, a_hi, a_lo], axis=1),
            jnp.concatenate([b_hi, b_lo, b_hi], axis=0),
            preferred_element_type=jnp.float32,
        )
    keep_ref[...] = total[:HALF]
    send_ref[...] = total[HALF:]


def product(place, a_parts, b_parts, by_row=False):
    tile = jax.ShapeDtypeStruct((HALF, WIDE), jnp.float32)
    anywhere = pl.BlockSpec(memory_space=pl.ANY)
    vmem = pl.BlockSpec(memory_space=pltpu.VMEM)
    return pl.pallas_call(
        functools.partial(product_kernel, by_row),
        out_shape=(tile, tile),
        in_specs=[pl.BlockSpec(memory_space=pltpu.SMEM)] + [anywhere] * (len(a_parts) + len(b_parts)),
        out_specs=(vmem, vmem),
        scratch_shapes=[
            pltpu.VMEM((2 * NZ, STRIP, HALF), jnp.float32),
            pltpu.VMEM((8, 2, HALF, WIDE), jnp.float32),
            pltpu.SemaphoreType.DMA((8,)),
            pltpu.SemaphoreType.DMA((8,)),
        ],
        compiler_params=pltpu.CompilerParams(vmem_limit_bytes=48 * 1024 * 1024),
        cost_estimate=pl.CostEstimate(
            flops=6 * STRIP * 2048 * WIDE, bytes_accessed=7 * 1024 * 1024, transcendentals=0
        ),
    )(place, *a_parts, *b_parts)


def sum_everywhere(first, second):
    parts = jnp.where(jnp.arange(HALF) == 0, first, second)
    mine = jnp.broadcast_to(parts, (NR * NZ * NC * NL, HALF))
    theirs = lax.all_to_all(mine, AXES, 0, 0, tiled=True)
    return jnp.sum(theirs, axis=0)[:STEPS]


def body(density, pattern):
    row, z = lax.axis_index("row"), lax.axis_index("z")
    core, layer = lax.axis_index("core"), lax.axis_index("layer")
    place = jnp.stack([row, z, core, layer]).astype(jnp.int32)
    first_core = core == 0
    strip_row = (row * NL + layer) * STRIP + core * HALF
    row_ids = strip_row + jnp.arange(HALF, dtype=jnp.int32)
    col_ids = z * WIDE + jnp.arange(WIDE, dtype=jnp.int32)
    blocks = jnp.arange(pattern.shape[0], dtype=jnp.int32)
    row_onehot = (row_ids[:, None] // BS == blocks[None, :]).astype(jnp.bfloat16)
    col_onehot = (blocks[:, None] == col_ids[None, :] // BS).astype(jnp.bfloat16)
    row_pattern = jnp.dot(
        row_onehot, pattern.astype(jnp.bfloat16), preferred_element_type=jnp.float32
    )
    occupied = (
        jnp.dot(row_pattern.astype(jnp.bfloat16), col_onehot, preferred_element_type=jnp.float32)
        > 0.5
    )
    on_diag = row_ids[:, None] == col_ids[None, :]

    near = lax.dynamic_slice_in_dim(density, layer * STRIP + core * HALF, HALF, 0)
    away = lax.dynamic_slice_in_dim(density, layer * STRIP + (1 - core) * HALF, HALF, 0)
    give = jnp.where(
        first_core,
        jnp.concatenate([away[:, HALF:], near[:, HALF:]], axis=0),
        jnp.concatenate([away[:, :HALF], near[:, :HALF]], axis=0),
    )
    a_mine = jnp.where(
        first_core,
        jnp.concatenate([near[:, :HALF], away[:, :HALF]], axis=0),
        jnp.concatenate([near[:, HALF:], away[:, HALF:]], axis=0),
    )
    a_other = swap(give)
    a_tile = jnp.where(
        first_core, jnp.stack([a_mine, a_other]), jnp.stack([a_other, a_mine])
    )
    density, a_tile = lax.optimization_barrier((density, a_tile))
    strips = density.reshape(NL, 2, HALF, STRIP)
    near = jnp.where(first_core, strips[:, 0], strips[:, 1])
    away = jnp.where(first_core, strips[:, 1], strips[:, 0])
    others = swap(away)
    b_tiles = jnp.where(
        first_core,
        jnp.concatenate([near, others], axis=2),
        jnp.concatenate([others, near], axis=2),
    )
    def diagonal(tile):
        return jnp.sum(jnp.where(on_diag, tile, jnp.zeros_like(tile)))

    a_parts = z_gather(a_tile)
    keep, send = product(place, a_parts, row_gather(b_tiles), by_row=True)
    total = keep + swap(send)
    square = jnp.where(occupied, total, jnp.zeros_like(total))
    keep, send = product(place, a_parts, plane_gather(square))
    total = keep + swap(send)
    cube_term = jnp.where(occupied, total, jnp.zeros_like(total))
    current = 3.0 * square - 2.0 * cube_term
    first_trace = diagonal(current)

    quarters = current.reshape(HALF, 4, HALF)
    low = jnp.stack([quarters[:, 0], quarters[:, 2]])
    high = jnp.stack([quarters[:, 1], quarters[:, 3]])
    mine = jnp.where(first_core, low, high)
    other = swap(jnp.where(first_core, high, low))
    a_tile = jnp.concatenate([mine, other], axis=1)
    a_tile, b_tile = lax.optimization_barrier((a_tile, current))
    a_parts = (lax.all_gather(a_tile, "z", axis=0, tiled=True),)
    b_parts = plane_gather(b_tile)
    keep, send = product(place, a_parts, b_parts)
    total = keep + swap(send)
    square = jnp.where(occupied, total, jnp.zeros_like(total))
    s_parts = plane_gather(square)
    keep, send = product(place, a_parts, s_parts)
    total = keep + swap(send)
    cube_term = jnp.where(occupied, total, jnp.zeros_like(total))
    current = 3.0 * square - 2.0 * cube_term

    traces = sum_everywhere(first_trace, diagonal(current))
    even, odd = current[:, :STRIP], current[:, STRIP:]
    mine = jnp.where(first_core, even, odd)
    other = swap(jnp.where(first_core, odd, even))
    tile = jnp.where(first_core, jnp.stack([mine, other]), jnp.stack([other, mine]))
    before = route(tile, lambda r, z, c, l: (r, z, c, l + 1))
    after = route(tile, lambda r, z, c, l: (r, z, c, l - 1))
    far = route(
        jnp.where(first_core, before, after),
        lambda r, z, c, l: (r, z, c, l + 1 - 2 * c),
    )
    stacked = jnp.stack([tile, after, far, before])
    purified = jnp.take(stacked, lax.rem(jnp.arange(NL) - layer + NL, NL), axis=0)
    return purified.reshape(NL * STRIP, STRIP), traces


def solution(mesh):
    fine = Mesh(mesh.devices.reshape(NR, NZ, NC, NL), AXES)
    placed = P("row", ("z", "core"))
    return jax.shard_map(
        body, mesh=fine, in_specs=(placed, P()), out_specs=(placed, P()), check_vma=False
    )
```

```python
import functools

import jax
import jax.numpy as jnp
from jax import lax
from jax.experimental import pallas as pl
from jax.experimental.pallas import tpu as pltpu
from jax.sharding import Mesh, PartitionSpec as P

BS = 64
STEPS = 2
AXES = ("row", "z", "core", "layer")
NR, NZ, NC, NL = 4, 8, 2, 4
STRIP = 256
HALF = 128
WIDE = 512


def route(value, step):
    pairs = []
    for r in range(NR):
        for z in range(NZ):
            for c in range(NC):
                for l in range(NL):
                    tr, tz, tc, tl = step(r, z, c, l)
                    target = (((tr % NR) * NZ + tz % NZ) * NC + tc) * NL + tl % NL
                    pairs.append((((r * NZ + z) * NC + c) * NL + l, target))
    return lax.ppermute(value, AXES, pairs)


def first_shift(value, by):
    return route(value, lambda r, z, c, l: (r + by * c, z, c, l + by * (1 - c)))


def second_shift(value, by):
    return route(value, lambda r, z, c, l: (r + by * (1 - c), z, c, l + by * c))


def z_shift(value, by):
    return route(value, lambda r, z, c, l: (r, z + by, c, l))


def swap(value):
    return route(value, lambda r, z, c, l: (r, z, 1 - c, l))


RING = (0, -1, 1, 2)
Z_OFFSETS = (0, -1, 1, -2, 2, -3, 3, 4)


def line_gather(low, high, shift):
    low_before, low_after = shift(low, 1), shift(low, -1)
    high_before, high_after = shift(high, 1), shift(high, -1)
    low_far, high_far = shift(low_before, 1), shift(high_after, -1)
    return low, high, low_before, high_before, low_after, high_after, low_far, high_far


def plane_gather(own):
    before, after, far = (first_shift(own, -place) for place in RING[1:])
    return line_gather(jnp.stack([own, before]), jnp.stack([after, far]), second_shift)


def row_gather(stacked):
    def shift(value, by):
        return route(value, lambda r, z, c, l: (r + by, z, c, l))

    before, after = shift(stacked, 1), shift(stacked, -1)
    return stacked, before, after, shift(before[:2], 1), shift(after[2:], -1)


def z_gather(own):
    before, after = z_shift(own, 1), z_shift(own, -1)
    before2, after2 = z_shift(before, 1), z_shift(after, -1)
    before3, after3 = z_shift(before2, 1), z_shift(after2, -1)
    first_core = lax.axis_index("core") == 0
    far = route(
        jnp.where(first_core, before3, after3),
        lambda r, z, c, l: (r, z + 1 - 2 * c, c, l),
    )
    return own, before, after, before2, after2, before3, after3, far


def split(value):
    hi = value.astype(jnp.bfloat16)
    lo = (value - hi.astype(jnp.float32)).astype(jnp.bfloat16)
    return hi, lo


def product_kernel(by_row, place_ref, *refs):
    b_count = 5 if by_row else 8
    a_refs, b_refs = refs[: -6 - b_count], refs[-6 - b_count : -6]
    keep_ref, send_ref, a_all, b_all, a_sem, b_sem = refs[-6:]
    row, z, core, layer = (place_ref[i] for i in range(4))
    a_copies = []
    if len(a_refs) == 1:
        a_copies.append(pltpu.make_async_copy(a_refs[0], a_all, a_sem.at[0]))
        a_copies[-1].start()
    else:
        for i, offset in enumerate(Z_OFFSETS):
            at = lax.rem(z + offset + NZ, NZ)
            a_copies.append(
                pltpu.make_async_copy(a_refs[i], a_all.at[pl.ds(2 * at, 2)], a_sem.at[i])
            )
            a_copies[-1].start()
    b_copies = []
    for i in range(8):
        if not by_row:
            ref = b_refs[i]
        else:
            ref = b_refs[i // 2].at[pl.ds(2 * (i % 2), 2)] if i < 6 else b_refs[i - 3]
        b_copies.append(pltpu.make_async_copy(ref, b_all.at[i], b_sem.at[i]))
        b_copies[-1].start()
    for copy in a_copies:
        copy.wait()
    total = jnp.zeros((STRIP, WIDE), jnp.float32)
    for i in range(8):
        second = RING[i // 2]
        b_copies[i].wait()
        a_parts = []
        for slot in (2 * (i % 2), 2 * (i % 2) + 1):
            if by_row:
                strip = lax.rem(row + second + NR, NR) * NL + slot
            else:
                first = RING[slot]
                row_offset = jnp.where(core == 0, second, first)
                layer_offset = jnp.where(core == 0, first, second)
                strip = lax.rem(row + row_offset + NR, NR) * NL + lax.rem(
                    layer + layer_offset + NL, NL
                )
            a_parts.append(a_all[strip])
        a_hi, a_lo = split(jnp.concatenate(a_parts, axis=1))
        b_hi, b_lo = split(b_all[i].reshape(STRIP, WIDE))
        total += jnp.dot(
            jnp.concatenate([a_hi, a_hi, a_lo], axis=1),
            jnp.concatenate([b_hi, b_lo, b_hi], axis=0),
            preferred_element_type=jnp.float32,
        )
    keep_ref[...] = total[:HALF]
    send_ref[...] = total[HALF:]


def product(place, a_parts, b_parts, by_row=False):
    tile = jax.ShapeDtypeStruct((HALF, WIDE), jnp.float32)
    anywhere = pl.BlockSpec(memory_space=pl.ANY)
    vmem = pl.BlockSpec(memory_space=pltpu.VMEM)
    return pl.pallas_call(
        functools.partial(product_kernel, by_row),
        out_shape=(tile, tile),
        in_specs=[pl.BlockSpec(memory_space=pltpu.SMEM)] + [anywhere] * (len(a_parts) + len(b_parts)),
        out_specs=(vmem, vmem),
        scratch_shapes=[
            pltpu.VMEM((2 * NZ, STRIP, HALF), jnp.float32),
            pltpu.VMEM((8, 2, HALF, WIDE), jnp.float32),
            pltpu.SemaphoreType.DMA((8,)),
            pltpu.SemaphoreType.DMA((8,)),
        ],
        compiler_params=pltpu.CompilerParams(vmem_limit_bytes=50 * 1024 * 1024),
        cost_estimate=pl.CostEstimate(
            flops=6 * STRIP * 2048 * WIDE, bytes_accessed=7 * 1024 * 1024, transcendentals=0
        ),
    )(place, *a_parts, *b_parts)


def sum_everywhere(first, second):
    parts = jnp.where(jnp.arange(HALF) == 0, first, second)
    mine = jnp.broadcast_to(parts, (NR * NZ * NC * NL, HALF))
    theirs = lax.all_to_all(mine, AXES, 0, 0, tiled=True)
    return jnp.sum(theirs, axis=0)[:STEPS]


def body(density, pattern):
    row, z = lax.axis_index("row"), lax.axis_index("z")
    core, layer = lax.axis_index("core"), lax.axis_index("layer")
    place = jnp.stack([row, z, core, layer]).astype(jnp.int32)
    first_core = core == 0
    strip_row = (row * NL + layer) * STRIP + core * HALF
    row_ids = strip_row + jnp.arange(HALF, dtype=jnp.int32)
    col_ids = z * WIDE + jnp.arange(WIDE, dtype=jnp.int32)
    blocks = jnp.arange(pattern.shape[0], dtype=jnp.int32)
    row_onehot = (row_ids[:, None] // BS == blocks[None, :]).astype(jnp.bfloat16)
    col_onehot = (blocks[:, None] == col_ids[None, :] // BS).astype(jnp.bfloat16)
    row_pattern = jnp.dot(
        row_onehot, pattern.astype(jnp.bfloat16), preferred_element_type=jnp.float32
    )
    occupied = (
        jnp.dot(row_pattern.astype(jnp.bfloat16), col_onehot, preferred_element_type=jnp.float32)
        > 0.5
    )
    on_diag = row_ids[:, None] == col_ids[None, :]

    near = lax.dynamic_slice_in_dim(density, layer * STRIP + core * HALF, HALF, 0)
    away = lax.dynamic_slice_in_dim(density, layer * STRIP + (1 - core) * HALF, HALF, 0)
    give = jnp.where(
        first_core,
        jnp.concatenate([away[:, HALF:], near[:, HALF:]], axis=0),
        jnp.concatenate([away[:, :HALF], near[:, :HALF]], axis=0),
    )
    a_mine = jnp.where(
        first_core,
        jnp.concatenate([near[:, :HALF], away[:, :HALF]], axis=0),
        jnp.concatenate([near[:, HALF:], away[:, HALF:]], axis=0),
    )
    a_other = swap(give)
    a_tile = jnp.where(
        first_core, jnp.stack([a_mine, a_other]), jnp.stack([a_other, a_mine])
    )
    density, a_tile = lax.optimization_barrier((density, a_tile))
    strips = density.reshape(NL, 2, HALF, STRIP)
    near = jnp.where(first_core, strips[:, 0], strips[:, 1])
    away = jnp.where(first_core, strips[:, 1], strips[:, 0])
    others = swap(away)
    b_tiles = jnp.where(
        first_core,
        jnp.concatenate([near, others], axis=2),
        jnp.concatenate([others, near], axis=2),
    )
    def diagonal(tile):
        return jnp.sum(jnp.where(on_diag, tile, jnp.zeros_like(tile)))

    a_parts = z_gather(a_tile)
    keep, send = product(place, a_parts, row_gather(b_tiles), by_row=True)
    total = keep + swap(send)
    square = jnp.where(occupied, total, jnp.zeros_like(total))
    keep, send = product(place, a_parts, plane_gather(square))
    total = keep + swap(send)
    cube_term = jnp.where(occupied, total, jnp.zeros_like(total))
    current = 3.0 * square - 2.0 * cube_term
    first_trace = diagonal(current)

    quarters = current.reshape(HALF, 4, HALF)
    low = jnp.stack([quarters[:, 0], quarters[:, 2]])
    high = jnp.stack([quarters[:, 1], quarters[:, 3]])
    mine = jnp.where(first_core, low, high)
    other = swap(jnp.where(first_core, high, low))
    a_tile = jnp.concatenate([mine, other], axis=1)
    a_tile, b_tile = lax.optimization_barrier((a_tile, current))
    a_parts = (lax.all_gather(a_tile, "z", axis=0, tiled=True),)
    b_parts = plane_gather(b_tile)
    keep, send = product(place, a_parts, b_parts)
    total = keep + swap(send)
    square = jnp.where(occupied, total, jnp.zeros_like(total))
    s_parts = plane_gather(square)
    keep, send = product(place, a_parts, s_parts)
    total = keep + swap(send)
    cube_term = jnp.where(occupied, total, jnp.zeros_like(total))
    current = 3.0 * square - 2.0 * cube_term

    traces = sum_everywhere(first_trace, diagonal(current))
    even, odd = current[:, :STRIP], current[:, STRIP:]
    mine = jnp.where(first_core, even, odd)
    other = swap(jnp.where(first_core, odd, even))
    tile = jnp.where(first_core, jnp.stack([mine, other]), jnp.stack([other, mine]))
    before = route(tile, lambda r, z, c, l: (r, z, c, l + 1))
    after = route(tile, lambda r, z, c, l: (r, z, c, l - 1))
    far = route(
        jnp.where(first_core, before, after),
        lambda r, z, c, l: (r, z, c, l + 1 - 2 * c),
    )
    stacked = jnp.stack([tile, after, far, before])
    purified = jnp.take(stacked, lax.rem(jnp.arange(NL) - layer + NL, NL), axis=0)
    return purified.reshape(NL * STRIP, STRIP), traces


def solution(mesh):
    fine = Mesh(mesh.devices.reshape(NR, NZ, NC, NL), AXES)
    placed = P("row", ("z", "core"))
    return jax.shard_map(
        body, mesh=fine, in_specs=(placed, P()), out_specs=(placed, P()), check_vma=False
    )
```
